512 devices in a mesh: row: 8 (over z_lo), col: 8 (over x, core), depth: 8 (over y, z_hi).
Axes of the slice: x: 4, y: 4, z: 16 (z_hi: 2, z_lo: 8; z = z_hi * 8 + z_lo), core: 2. Of those that a mesh axis runs over, the one named last changes fastest.
Arguments:
- tokens: bfloat16 [512, 7424], P(('col', 'depth'), 'row'), may hold values from -6 to 6
- out_grad: bfloat16 [512, 7424], P(('col', 'depth'), 'row'), may hold values from -1.5 to 1.5
- up_weight: bfloat16 [7424, 29696], P('row', ('col', 'depth')), may hold values from -0.0625 to 0.0625
- down_weight: bfloat16 [29696, 7424], P(('col', 'depth'), 'row'), may hold values from -0.03125 to 0.03125
Outputs:
- token_grad: bfloat16 [512, 7424], P(('col', 'depth'), 'row')
- up_grad: float32 [7424, 29696], P('row', ('col', 'depth'))
- down_grad: float32 [29696, 7424], P(('col', 'depth'), 'row')
The draws below stay inside these ranges and needn't reach their ends.
All inputs are finite; a program needn't handle non-finite values.
Results may differ from the reference program's by a relative error of at most 0.024.
Values may be sent and summed in bfloat16 or wider, within the bound.
No kernel may reach another device: no remote copies, remote signals or barrier semaphores. Data moves between devices by JAX's collectives and lax.ppermute only.
A program may use at most 192 MiB of HBM per device.

```python
import jax
import jax.numpy as jnp
from jax import lax

D = 7424
FF = 29696
TOK_DEV = 8
TOKENS = 512
N_ROW = 8
N_COL = 8
N_DEPTH = 8


def shard_levels(own_key, dims, cuts, low, high):
    def one(axis_at, shards_of):
        draws = jax.random.uniform(jax.random.fold_in(jax.random.fold_in(own_key, 6), axis_at), (shards_of,), jnp.float32, low / len(cuts), high / len(cuts))
        return jnp.repeat(jnp.exp(draws), dims[axis_at] // shards_of).reshape((-1,) + (1,) * (len(dims) - axis_at - 1))

    loudness = one(*cuts[0])
    for cut in cuts[1:]:
        loudness = loudness * one(*cut)
    return loudness


def normal_values(stream_key, dims, spread, reach, shards=(), dtype=jnp.bfloat16):
    array = jax.random.normal(stream_key, dims, jnp.float32) * spread
    if len(shards) > 0:
        array = shard_levels(stream_key, dims, shards, -0.22, 0.18) * array
    return jnp.clip(array, min=-reach, max=reach).astype(dtype)


def setup_inputs(seed: int = 0) -> dict:
    streams_of = jax.random.split(jax.random.key(seed), 5)
    return {
        "tokens": normal_values(streams_of[0], (TOKENS, D), 1.0, 6.0, ((0, 64), (1, 8))),
        "out_grad": normal_values(streams_of[1], (TOKENS, D), 0.25, 1.5, ((0, 64), (1, 8))),
        "up_weight": normal_values(streams_of[2], (D, FF), D ** -0.5, 0.0625, ((0, 8), (1, 64))),
        "down_weight": normal_values(streams_of[3], (FF, D), FF ** -0.5, 0.03125, ((0, 64), (1, 8))),
    }


def gelu_slope(preact):
    normal_cdf = 0.5 * (1.0 + lax.erf(preact * 0.7071067811865476))
    return normal_cdf + preact * jnp.exp(-0.5 * preact * preact) * 0.3989422804014327


def rounded(partial_value):
    return lax.optimization_barrier(partial_value.astype(jnp.bfloat16)).astype(jnp.float32)


def grouped_product(leading, trailing, groups):
    group_width = leading.shape[1] // groups
    running = jnp.zeros((leading.shape[0], trailing.shape[1]), jnp.float32)
    for group_index in range(groups):
        offset = group_index * group_width
        partial_value = jnp.dot(leading[:, offset:offset + group_width], trailing[offset:offset + group_width], preferred_element_type=jnp.float32)
        running = running + rounded(partial_value)
    return running


def reference(tokens, out_grad, up_weight, down_weight):
    preact = grouped_product(tokens, up_weight, N_ROW)
    active = jax.nn.gelu(preact, approximate=False).astype(jnp.bfloat16)
    grad_active = grouped_product(out_grad, down_weight.T, N_ROW)
    grad_preact = (grad_active * gelu_slope(preact)).astype(jnp.bfloat16)
    token_grad = jnp.dot(grad_preact, up_weight.T, preferred_element_type=jnp.float32).astype(jnp.bfloat16)
    inputs_four = tokens.reshape(N_COL, N_DEPTH, TOK_DEV, D)
    upstream_four = out_grad.reshape(N_COL, N_DEPTH, TOK_DEV, D)
    active_four = active.reshape(N_COL, N_DEPTH, TOK_DEV, FF)
    hidden_four = grad_preact.reshape(N_COL, N_DEPTH, TOK_DEV, FF)
    up_grad = jnp.zeros((D, FF), jnp.float32)
    down_grad = jnp.zeros((FF, D), jnp.float32)
    for group_index in range(N_DEPTH):
        inputs_group = inputs_four[:, group_index].reshape(N_COL * TOK_DEV, D)
        upstream_group = upstream_four[:, group_index].reshape(N_COL * TOK_DEV, D)
        active_group = active_four[:, group_index].reshape(N_COL * TOK_DEV, FF)
        hidden_group = hidden_four[:, group_index].reshape(N_COL * TOK_DEV, FF)
        up_grad = up_grad + rounded(jnp.dot(inputs_group.T, hidden_group, preferred_element_type=jnp.float32))
        down_grad = down_grad + rounded(jnp.dot(active_group.T, upstream_group, preferred_element_type=jnp.float32))
    return token_grad, up_grad, down_grad
```

```python
import jax
import jax.numpy as jnp
from jax import lax
from jax.sharding import Mesh, PartitionSpec as P

AXES = ("za", "zb", "zc", "x", "core", "y", "far")
SIZES = (2, 2, 2, 4, 2, 4, 2)
ROW = ("za", "zb", "zc")
TOKENS_OVER = ("x", "core", "y", "far")
SWAP = [(0, 1), (1, 0)]


def gelu_cdf(preact):
    return 0.5 * (1.0 + lax.erf(preact * 0.7071067811865476))


def against(leading, trailing):
    return lax.dot_general(
        leading, trailing, (((1,), (1,)), ((), ())), preferred_element_type=jnp.float32
    )


def weight_grad(leading, trailing):
    return lax.dot_general(
        leading, trailing, (((0,), (0,)), ((), ())), preferred_element_type=jnp.float32
    )


def exchange_sum(blocks, axis):
    swapped = lax.all_to_all(blocks, axis, split_axis=0, concat_axis=0, tiled=True)
    return jnp.sum(swapped.astype(jnp.float32), axis=0)


def on_device(tokens, out_grad, up_weight, down_weight):
    rows, features = tokens.shape
    hidden = up_weight.shape[1]
    with jax.named_scope("gather_tokens"):
        own = jnp.concatenate([tokens, out_grad], axis=0)
        for axis in ("far", "y", "x"):
            own = lax.all_gather(own, axis, axis=0, tiled=True)
        other = lax.ppermute(own, "core", SWAP)
        own = own.reshape(-1, 2, rows, features)
        other = other.reshape(-1, 2, rows, features)
        inputs, upstream = (
            jnp.concatenate([own[:, i], other[:, i]], axis=0).reshape(-1, features)
            for i in range(2)
        )
    with jax.named_scope("row_sum"):
        partials = jnp.stack(
            [
                jnp.dot(inputs, up_weight, preferred_element_type=jnp.float32)
                .astype(jnp.bfloat16)
                .reshape(8, -1, hidden),
                against(upstream, down_weight).astype(jnp.bfloat16).reshape(8, -1, hidden),
            ],
            axis=1,
        )
        share = partials.shape[2]
        quarter = exchange_sum(partials.reshape(4, 2, 2, share, hidden), ("zb", "zc"))
        sums = exchange_sum(quarter.astype(jnp.bfloat16), "za")
    with jax.named_scope("activate"):
        preact, grad_active = sums[0], sums[1]
        cdf = gelu_cdf(preact)
        slope = cdf + preact * jnp.exp(-0.5 * preact * preact) * 0.3989422804014327
        both = jnp.stack([preact * cdf, grad_active * slope]).astype(jnp.bfloat16)[None]
    with jax.named_scope("row_gather"):
        both = lax.all_gather(both, "za", axis=0, tiled=True)
        both = lax.all_gather(both, ("zb", "zc"), axis=0, tiled=True)
        active = both[:, 0].reshape(-1, hidden)
        hidden_grad = both[:, 1].reshape(-1, hidden)
    with jax.named_scope("token_grad"):
        partial_grad = against(hidden_grad, up_weight).reshape(2, -1, features)
        arrived = lax.ppermute(partial_grad[1].astype(jnp.bfloat16), "core", SWAP)
        chip_sum = (partial_grad[0] + arrived.astype(jnp.float32)).astype(jnp.bfloat16)
        x_sum = exchange_sum(chip_sum.reshape(4, -1, features), "x").astype(jnp.bfloat16)
        token_grad = exchange_sum(x_sum.reshape(8, -1, features), ("y", "far"))
    with jax.named_scope("weight_grads"):
        up_grad = weight_grad(inputs, hidden_grad)
        down_grad = weight_grad(active, upstream)
    return (token_grad.astype(jnp.bfloat16), up_grad, down_grad)


def solution(mesh):
    fine = Mesh(mesh.devices.reshape(SIZES), AXES)
    return jax.shard_map(
        on_device,
        mesh=fine,
        in_specs=(P(TOKENS_OVER, ROW), P(TOKENS_OVER, ROW), P(ROW, TOKENS_OVER), P(TOKENS_OVER, ROW)),
        out_specs=(P(TOKENS_OVER, ROW), P(ROW, TOKENS_OVER), P(TOKENS_OVER, ROW)),
        check_vma=False,
    )
```

```python
import functools

import jax
import jax.numpy as jnp
from jax import lax
from jax.experimental import pallas as pl
from jax.experimental.pallas import tpu as pltpu
from jax.sharding import Mesh, PartitionSpec as P

AXES = ("za", "zb", "zc", "x", "core", "y", "far")
SIZES = (2, 2, 2, 4, 2, 4, 2)
ROW = ("za", "zb", "zc")
TOKENS_OVER = ("x", "core", "y", "far")
SWAP = [(0, 1), (1, 0)]


def gelu_cdf(preact):
    return 0.5 * (1.0 + lax.erf(preact * 0.7071067811865476))


VMEM = pl.BlockSpec(memory_space=pltpu.VMEM)


def on_core(kernel, out_shape, flops, *operands):
    nbytes = 2 * sum(x.size for x in operands)
    return pl.pallas_call(
        kernel,
        out_shape=out_shape,
        in_specs=[VMEM] * len(operands),
        out_specs=[VMEM] * len(out_shape),
        compiler_params=pltpu.CompilerParams(vmem_limit_bytes=24 << 20),
        cost_estimate=pl.CostEstimate(flops=flops, bytes_accessed=nbytes, transcendentals=0),
    )(*operands)


def partials_kernel(own_ref, other_ref, up_ref, down_ref, parts_ref, inputs_ref, upstream_ref):
    for half, ref in enumerate((own_ref, other_ref)):
        for piece in range(2):
            block = 2 * half + piece
            rows = pl.ds(128 * block, 128)
            tokens = ref[8 * piece : 8 * piece + 8, 0].reshape(128, -1)
            grads = ref[8 * piece : 8 * piece + 8, 1].reshape(128, -1)
            inputs_ref[rows] = tokens
            upstream_ref[rows] = grads
            parts_ref[block, 0] = lax.dot_general(
                up_ref[...], tokens, (((0,), (1,)), ((), ())), preferred_element_type=jnp.float32
            ).astype(jnp.bfloat16)
            parts_ref[block, 1] = lax.dot_general(
                down_ref[...], grads, (((1,), (1,)), ((), ())), preferred_element_type=jnp.float32
            ).astype(jnp.bfloat16)


def token_grad_kernel(first, both_ref, up_ref, out_ref):
    for piece in range(2):
        out_ref[pl.ds(128 * piece, 128)] = lax.dot_general(
            both_ref[first + piece, 1],
            up_ref[...],
            (((0,), (1,)), ((), ())),
            preferred_element_type=jnp.float32,
        ).astype(jnp.bfloat16)


def total(blocks):
    acc = blocks[0].astype(jnp.float32)
    for i in range(1, blocks.shape[0]):
        acc = acc + blocks[i].astype(jnp.float32)
    return acc


def exchange_sum(blocks, axis):
    return total(lax.all_to_all(blocks, axis, split_axis=0, concat_axis=0, tiled=True))


def on_device(tokens, out_grad, up_weight, down_weight):
    rows, features = tokens.shape
    hidden = up_weight.shape[1]
    with jax.named_scope("gather_tokens"):
        pair = lax.all_gather(jnp.stack([tokens, out_grad]), "far", axis=1, tiled=True)
        copies = jnp.broadcast_to(pair[None], (16,) + pair.shape)
        own = lax.all_to_all(copies, ("x", "y"), split_axis=0, concat_axis=0, tiled=True)
        other = lax.ppermute(own, "core", SWAP)
    with jax.named_scope("row_sum"):
        held = jax.ShapeDtypeStruct((512, features), jnp.bfloat16)
        parts, inputs, upstream = on_core(
            partials_kernel,
            [jax.ShapeDtypeStruct((4, 2, hidden, 128), jnp.bfloat16), held, held],
            4 * 512 * features * hidden,
            own,
            other,
            up_weight,
            down_weight,
        )
        quarter = exchange_sum(parts, ("zb", "zc")).astype(jnp.bfloat16)
        preact, grad_active = total(lax.all_gather(quarter, "za", axis=0, tiled=False))
    with jax.named_scope("activate"):
        cdf = 0.5 * (1.0 + lax.erf(preact * 0.7071067811865476))
        slope = cdf + preact * jnp.exp(-0.5 * preact * preact) * 0.3989422804014327
        both = jnp.stack([preact * cdf, grad_active * slope]).astype(jnp.bfloat16)
    with jax.named_scope("row_gather"):
        both = lax.all_gather(both[None], ("zb", "zc"), axis=0, tiled=True)
    with jax.named_scope("token_grad"):
        half = jax.ShapeDtypeStruct((256, features), jnp.bfloat16)
        flops = 2 * 256 * features * hidden
        leaving, staying = (
            on_core(functools.partial(token_grad_kernel, first), [half], flops, both, up_weight)[0]
            for first in (2, 0)
        )
        arrived = lax.ppermute(leaving, "core", SWAP)
        chip_sum = staying.astype(jnp.float32) + arrived.astype(jnp.float32)
        plane_sum = exchange_sum(
            chip_sum.astype(jnp.bfloat16).reshape(16, -1, features), ("x", "y")
        )
        token_grad = exchange_sum(
            plane_sum.astype(jnp.bfloat16).reshape(2, rows, features), "far"
        )
    with jax.named_scope("weight_grads"):
        up_grad = jnp.einsum(
            "btd,bht->dh",
            inputs.reshape(4, -1, features),
            both[:, 1],
            preferred_element_type=jnp.float32,
        )
        down_grad = jnp.einsum(
            "bht,btd->hd",
            both[:, 0],
            upstream.reshape(4, -1, features),
            preferred_element_type=jnp.float32,
        )
    return (token_grad.astype(jnp.bfloat16), up_grad, down_grad)


def solution(mesh):
    fine = Mesh(mesh.devices.reshape(SIZES), AXES)
    return jax.shard_map(
        on_device,
        mesh=fine,
        in_specs=(P(TOKENS_OVER, ROW), P(TOKENS_OVER, ROW), P(ROW, TOKENS_OVER), P(TOKENS_OVER, ROW)),
        out_specs=(P(TOKENS_OVER, ROW), P(ROW, TOKENS_OVER), P(TOKENS_OVER, ROW)),
        check_vma=False,
    )
```

```python
import functools

import jax
import jax.numpy as jnp
from jax import lax
from jax.experimental import pallas as pl
from jax.experimental.pallas import tpu as pltpu
from jax.sharding import Mesh, PartitionSpec as P

AXES = ("za", "zb", "zc", "x", "core", "y", "far")
SIZES = (2, 2, 2, 4, 2, 4, 2)
ROW = ("za", "zb", "zc")
TOKENS_OVER = ("x", "core", "y", "far")
SWAP = [(0, 1), (1, 0)]


def gelu_cdf(preact):
    return 0.5 * (1.0 + lax.erf(preact * 0.7071067811865476))


VMEM = pl.BlockSpec(memory_space=pltpu.VMEM)
ANY = pl.BlockSpec(memory_space=pl.ANY)
PARAMS = pltpu.CompilerParams(vmem_limit_bytes=24 << 20)


def on_core(kernel, out_shape, *operands):
    return pl.pallas_call(
        kernel,
        out_shape=out_shape,
        in_specs=[VMEM] * len(operands),
        out_specs=VMEM,
        compiler_params=PARAMS,
    )(*operands)


def in_order(kernel, out_shape, *operands, held_in=None):
    n = len(operands)
    later = operands[-1]
    passed = jax.ShapeDtypeStruct(later.shape, later.dtype)
    if held_in is not None:
        later = pltpu.with_memory_space_constraint(later, held_in)
        passed = held_in(passed.shape, passed.dtype)
    return pl.pallas_call(
        kernel,
        out_shape=[out_shape, passed],
        in_specs=[VMEM] * (n - 1) + [ANY],
        out_specs=[VMEM, ANY],
        input_output_aliases={n - 1: 1},
        compiler_params=PARAMS,
    )(*operands[:-1], later)


def total_then_kernel(blocks_ref, later_ref, out_ref, later_out_ref):
    total_kernel(blocks_ref, out_ref)


def partials_kernel(array, own_ref, other_ref, weight_ref, parts_ref, rows_ref):
    step = pl.program_id(0)

    def product(ref):
        rows = ref[pl.ds(8 * (step % 2), 8), array].reshape(128, -1)
        rows_ref[...] = rows
        parts_ref[0] = lax.dot_general(
            weight_ref[...],
            rows,
            (((array,), (1,)), ((), ())),
            preferred_element_type=jnp.float32,
        ).astype(jnp.bfloat16)

    @pl.when(step < 2)
    def _():
        product(own_ref)

    @pl.when(step >= 2)
    def _():
        product(other_ref)


def partials(array, own, other, weight):
    features = own.shape[3]
    hidden = weight.shape[1 - array]
    return pl.pallas_call(
        functools.partial(partials_kernel, array),
        grid=(4,),
        out_shape=[
            pltpu.HBM((4, hidden, 128), jnp.bfloat16),
            pltpu.HBM((512, features), jnp.bfloat16),
        ],
        in_specs=[VMEM, VMEM, VMEM],
        out_specs=[
            pl.BlockSpec((1, hidden, 128), lambda i: (i, 0, 0)),
            pl.BlockSpec((128, features), lambda i: (i, 0)),
        ],
        compiler_params=PARAMS,
    )(own, other, weight)


def token_grad_kernel(first, hidden_grad_ref, up_ref, out_ref):
    for piece in range(2):
        out_ref[pl.ds(128 * piece, 128)] = lax.dot_general(
            hidden_grad_ref[first + piece],
            up_ref[...],
            (((0,), (1,)), ((), ())),
            preferred_element_type=jnp.float32,
        ).astype(jnp.bfloat16)


def total_kernel(blocks_ref, out_ref):
    acc = blocks_ref[0].astype(jnp.float32)
    for i in range(1, blocks_ref.shape[0]):
        acc = acc + blocks_ref[i].astype(jnp.float32)
    out_ref[...] = acc.astype(jnp.bfloat16)


def add_kernel(*refs):
    acc = refs[0][...].astype(jnp.float32)
    for ref in refs[1:-1]:
        acc = acc + ref[...].astype(jnp.float32)
    refs[-1][...] = acc.astype(jnp.bfloat16)


def hidden_grad_kernel(mine_ref, theirs_ref, slope_ref, active_ref, out_ref, active_out_ref):
    grad_active = mine_ref[...].astype(jnp.float32) + theirs_ref[...].astype(jnp.float32)
    out_ref[...] = (grad_active * slope_ref[...]).astype(jnp.bfloat16)


def on_device(tokens, out_grad, up_weight, down_weight):
    rows, features = tokens.shape
    hidden = up_weight.shape[1]

    def exchange(blocks, axis):
        return lax.all_to_all(blocks, axis, split_axis=0, concat_axis=0, tiled=True)

    def row_gather(part):
        return lax.all_gather(part[None], ("zb", "zc"), axis=0, tiled=True)

    quarter = jax.ShapeDtypeStruct((hidden, 128), jnp.bfloat16)
    with jax.named_scope("gather_tokens"):
        pair = lax.all_gather(jnp.stack([tokens, out_grad]), "far", axis=1, tiled=True)
        copies = jnp.broadcast_to(pair[None], (16,) + pair.shape)
        own = exchange(copies, ("x", "y"))
        other = lax.ppermute(own, "core", SWAP)
    with jax.named_scope("row_sums"):
        pre_parts, inputs = partials(0, own, other, up_weight)
        grad_parts, upstream = partials(1, own, other, down_weight)
        pre_mine, grad_parts = in_order(
            total_then_kernel,
            quarter,
            exchange(pre_parts, ("zb", "zc")),
            grad_parts,
            held_in=pltpu.HBM,
        )
        pre_theirs = lax.ppermute(pre_mine, "za", SWAP)
        grad_mine = on_core(total_kernel, quarter, exchange(grad_parts, ("zb", "zc")))
        grad_theirs = lax.ppermute(grad_mine, "za", SWAP)
    with jax.named_scope("activate"):
        preact = pre_mine.astype(jnp.float32) + pre_theirs.astype(jnp.float32)
        cdf = 0.5 * (1.0 + lax.erf(preact * 0.7071067811865476))
        slope = cdf + preact * jnp.exp(-0.5 * preact * preact) * 0.3989422804014327
        active = row_gather((preact * cdf).astype(jnp.bfloat16))
        hidden_grad, active = in_order(
            hidden_grad_kernel, quarter, grad_mine, grad_theirs, slope, active
        )
        hidden_grad = row_gather(hidden_grad)
    with jax.named_scope("token_grad"):
        half = jax.ShapeDtypeStruct((256, features), jnp.bfloat16)
        leaving, staying = (
            on_core(functools.partial(token_grad_kernel, first), half, hidden_grad, up_weight)
            for first in (2, 0)
        )
        arrived = lax.ppermute(leaving, "core", SWAP)
        chip_sum = on_core(add_kernel, half, staying, arrived)
        plane_sum = on_core(
            total_kernel,
            jax.ShapeDtypeStruct((2 * rows, features), jnp.bfloat16),
            exchange(chip_sum.reshape(16, -1, features), ("x", "y")),
        )
        both_sums = lax.all_gather(plane_sum, "far", axis=0, tiled=False)
        own_rows = lax.dynamic_slice_in_dim(
            both_sums, rows * lax.axis_index("far"), rows, axis=1
        ).astype(jnp.float32)
        token_grad = own_rows[0] + own_rows[1]
    with jax.named_scope("weight_grads"):
        up_grad = jnp.einsum(
            "btd,bht->dh",
            inputs.reshape(4, -1, features),
            hidden_grad,
            preferred_element_type=jnp.float32,
        )
        down_grad = jnp.einsum(
            "bht,btd->hd",
            active,
            upstream.reshape(4, -1, features),
            preferred_element_type=jnp.float32,
        )
    return (token_grad.astype(jnp.bfloat16), up_grad, down_grad)


def solution(mesh):
    fine = Mesh(mesh.devices.reshape(SIZES), AXES)
    return jax.shard_map(
        on_device,
        mesh=fine,
        in_specs=(P(TOKENS_OVER, ROW), P(TOKENS_OVER, ROW), P(ROW, TOKENS_OVER), P(TOKENS_OVER, ROW)),
        out_specs=(P(TOKENS_OVER, ROW), P(ROW, TOKENS_OVER), P(TOKENS_OVER, ROW)),
        check_vma=False,
    )
```

```python
import functools

import jax
import jax.numpy as jnp
from jax import lax
from jax.experimental import pallas as pl
from jax.experimental.pallas import tpu as pltpu
from jax.sharding import Mesh, PartitionSpec as P

AXES = ("za", "zb", "zc", "x", "core", "y", "far")
SIZES = (2, 2, 2, 4, 2, 4, 2)
ROW = ("za", "zb", "zc")
TOKENS_OVER = ("x", "core", "y", "far")
SWAP = [(0, 1), (1, 0)]


def gelu_cdf(preact):
    return 0.5 * (1.0 + lax.erf(preact * 0.7071067811865476))


VMEM = pl.BlockSpec(memory_space=pltpu.VMEM)
ANY = pl.BlockSpec(memory_space=pl.ANY)
PARAMS = pltpu.CompilerParams(vmem_limit_bytes=24 << 20)


def on_core(kernel, out_shape, *operands):
    return pl.pallas_call(
        kernel,
        out_shape=out_shape,
        in_specs=[VMEM] * len(operands),
        out_specs=VMEM,
        compiler_params=PARAMS,
    )(*operands)


def in_order(kernel, out_shape, *operands):
    n = len(operands)
    later = operands[-1]
    return pl.pallas_call(
        kernel,
        out_shape=[out_shape, jax.ShapeDtypeStruct(later.shape, later.dtype)],
        in_specs=[VMEM] * (n - 1) + [ANY],
        out_specs=[VMEM, ANY],
        input_output_aliases={n - 1: 1},
        compiler_params=PARAMS,
    )(*operands)


def partials_kernel(plane_ref, up_ref, down_ref, *refs):
    parts_ref, inputs_ref, upstream_ref = refs[-3:]
    step = pl.program_id(0)
    for array, (weight_ref, rows_ref) in enumerate(
        ((up_ref, inputs_ref), (down_ref, upstream_ref))
    ):
        rows = plane_ref[pl.ds(8 * step, 8), array].reshape(128, -1)
        rows_ref[...] = rows
        parts_ref[0, array] = lax.dot_general(
            weight_ref[...],
            rows,
            (((array,), (1,)), ((), ())),
            preferred_element_type=jnp.float32,
        ).astype(jnp.bfloat16)


def partials(half, plane, up_weight, down_weight, *so_far):
    features, hidden = up_weight.shape
    return pl.pallas_call(
        partials_kernel,
        grid=(2,),
        out_shape=[
            jax.ShapeDtypeStruct((4, 2, hidden, 128), jnp.bfloat16),
            pltpu.HBM((512, features), jnp.bfloat16),
            pltpu.HBM((512, features), jnp.bfloat16),
        ],
        in_specs=[VMEM] * 3 + [ANY] * len(so_far),
        out_specs=[
            pl.BlockSpec((1, 2, hidden, 128), lambda i: (2 * half + i, 0, 0, 0)),
            pl.BlockSpec((128, features), lambda i: (2 * half + i, 0)),
            pl.BlockSpec((128, features), lambda i: (2 * half + i, 0)),
        ],
        input_output_aliases={3 + i: i for i in range(len(so_far))},
        compiler_params=PARAMS,
        cost_estimate=pl.CostEstimate(
            flops=2 * 512 * features * hidden, bytes_accessed=4 << 20, transcendentals=0
        ),
    )(plane, up_weight, down_weight, *so_far)


def token_grad_kernel(first, hidden_grad_ref, up_ref, *refs):
    out_ref = refs[-2] if len(refs) == 3 else refs[0]
    for piece in range(2):
        out_ref[pl.ds(128 * piece, 128)] = lax.dot_general(
            hidden_grad_ref[first + piece],
            up_ref[...],
            (((0,), (1,)), ((), ())),
            preferred_element_type=jnp.float32,
        ).astype(jnp.bfloat16)


def total_kernel(blocks_ref, out_ref):
    acc = blocks_ref[0].astype(jnp.float32)
    for i in range(1, blocks_ref.shape[0]):
        acc = acc + blocks_ref[i].astype(jnp.float32)
    out_ref[...] = acc.astype(jnp.bfloat16)


def add_kernel(*refs):
    acc = refs[0][...].astype(jnp.float32)
    for ref in refs[1:-1]:
        acc = acc + ref[...].astype(jnp.float32)
    refs[-1][...] = acc.astype(jnp.bfloat16)


def weight_grads_kernel(
    place_ref,
    inputs_ref,
    upstream_ref,
    hidden_grad_ref,
    *refs,
):
    parts, (up_out, down_out, active_ref, up_ref, down_ref, sems) = refs[:4], refs[4:]

    def whole(ref):
        return jnp.concatenate([ref[i] for i in range(4)], axis=1)

    copies = [
        pltpu.make_async_copy(up_ref, up_out, sems.at[0]),
        pltpu.make_async_copy(down_ref, down_out, sems.at[1]),
    ]
    up_ref[...] = lax.dot_general(
        inputs_ref[...],
        whole(hidden_grad_ref),
        (((0,), (1,)), ((), ())),
        preferred_element_type=jnp.float32,
    )
    copies[0].start()
    for k in range(4):
        active_ref[place_ref[0] ^ k] = parts[k][...]
    down_ref[...] = jnp.dot(
        whole(active_ref), upstream_ref[...], preferred_element_type=jnp.float32
    )
    copies[1].start()
    for copy in copies:
        copy.wait()


def weight_grads(place, inputs, upstream, hidden_grad, active_parts):
    tokens, features = inputs.shape
    hidden = hidden_grad.shape[1]
    up = (features, hidden)
    down = (hidden, features)
    return pl.pallas_call(
        weight_grads_kernel,
        out_shape=[pltpu.HBM(up, jnp.float32), pltpu.HBM(down, jnp.float32)],
        in_specs=[pl.BlockSpec(memory_space=pltpu.SMEM)] + [VMEM] * 7,
        out_specs=[ANY, ANY],
        scratch_shapes=[
            pltpu.VMEM(hidden_grad.shape, jnp.bfloat16),
            pltpu.VMEM(up, jnp.float32),
            pltpu.VMEM(down, jnp.float32),
            pltpu.SemaphoreType.DMA((2,)),
        ],
        compiler_params=PARAMS,
        cost_estimate=pl.CostEstimate(
            flops=4 * tokens * features * hidden, bytes_accessed=8 << 20, transcendentals=0
        ),
    )(place.reshape(1), inputs, upstream, hidden_grad, *active_parts)


def on_device(tokens, out_grad, up_weight, down_weight):
    rows, features = tokens.shape
    hidden = up_weight.shape[1]

    def exchange(blocks, axis):
        return lax.all_to_all(blocks, axis, split_axis=0, concat_axis=0, tiled=True)

    def row_gather(part):
        return lax.all_gather(part[None], ("zb", "zc"), axis=0, tiled=True)

    with jax.named_scope("gather_tokens"):
        pair = lax.all_gather(jnp.stack([tokens, out_grad]), "far", axis=1, tiled=True)
        copies = jnp.broadcast_to(pair[None], (16,) + pair.shape)
        own = exchange(copies, ("x", "y"))
        other = lax.ppermute(own, "core", SWAP)
    with jax.named_scope("row_sums"):
        first = partials(0, own, up_weight, down_weight)
        parts, inputs, upstream = partials(1, other, up_weight, down_weight, *first)
        place = lax.axis_index(("zb", "zc"))
        quarter = jax.ShapeDtypeStruct((hidden, 128), jnp.bfloat16)
        sums = []
        for array in range(2):
            pieces = [
                lax.dynamic_index_in_dim(parts[:, array], place ^ k, 0, keepdims=False)
                for k in range(4)
            ]
            for k in (1, 2, 3):
                pieces[k] = lax.ppermute(
                    pieces[k], ("zb", "zc"), [(i, i ^ k) for i in range(4)]
                )
            mine = on_core(add_kernel, quarter, *pieces)
            theirs = lax.ppermute(mine, "za", SWAP)
            sums.append(mine.astype(jnp.float32) + theirs.astype(jnp.float32))
        preact, grad_active = sums
    with jax.named_scope("activate"):
        cdf = 0.5 * (1.0 + lax.erf(preact * 0.7071067811865476))
        slope = cdf + preact * jnp.exp(-0.5 * preact * preact) * 0.3989422804014327
        hidden_grad = row_gather((grad_active * slope).astype(jnp.bfloat16))
        active = (preact * cdf).astype(jnp.bfloat16)
    with jax.named_scope("token_grad"):
        half = jax.ShapeDtypeStruct((256, features), jnp.bfloat16)
        leaving, active = in_order(
            functools.partial(token_grad_kernel, 2), half, hidden_grad, up_weight, active
        )
        staying = on_core(functools.partial(token_grad_kernel, 0), half, hidden_grad, up_weight)
        arrived = lax.ppermute(leaving, "core", SWAP)
        chip_sum = on_core(add_kernel, half, staying, arrived)
        plane_sum = on_core(
            total_kernel,
            jax.ShapeDtypeStruct((2 * rows, features), jnp.bfloat16),
            exchange(chip_sum.reshape(16, -1, features), ("x", "y")),
        )
        far = lax.axis_index("far")
        mine, theirs = (
            lax.dynamic_slice_in_dim(plane_sum, rows * side, rows, axis=0)
            for side in (far, 1 - far)
        )
        token_grad = on_core(
            add_kernel,
            jax.ShapeDtypeStruct((rows, features), jnp.bfloat16),
            mine,
            lax.ppermute(theirs, "far", SWAP),
        )
    with jax.named_scope("weight_grads"):
        place = lax.axis_index(("zb", "zc"))
        active_parts = [active] + [
            lax.ppermute(active, ("zb", "zc"), [(i, i ^ k) for i in range(4)])
            for k in (1, 2, 3)
        ]
        up_grad, down_grad = weight_grads(place, inputs, upstream, hidden_grad, active_parts)
    return (token_grad, up_grad, down_grad)


def solution(mesh):
    fine = Mesh(mesh.devices.reshape(SIZES), AXES)
    return jax.shard_map(
        on_device,
        mesh=fine,
        in_specs=(P(TOKENS_OVER, ROW), P(TOKENS_OVER, ROW), P(ROW, TOKENS_OVER), P(TOKENS_OVER, ROW)),
        out_specs=(P(TOKENS_OVER, ROW), P(ROW, TOKENS_OVER), P(TOKENS_OVER, ROW)),
        check_vma=False,
    )
```

```python
import functools

import jax
import jax.numpy as jnp
from jax import lax
from jax.experimental import pallas as pl
from jax.experimental.pallas import tpu as pltpu
from jax.sharding import Mesh, PartitionSpec as P

AXES = ("za", "zb", "zc", "x", "core", "y", "far")
SIZES = (2, 2, 2, 4, 2, 4, 2)
ROW = ("za", "zb", "zc")
TOKENS_OVER = ("x", "core", "y", "far")
SWAP = [(0, 1), (1, 0)]


def gelu_cdf(preact):
    return 0.5 * (1.0 + lax.erf(preact * 0.7071067811865476))


VMEM = pl.BlockSpec(memory_space=pltpu.VMEM)
ANY = pl.BlockSpec(memory_space=pl.ANY)
PARAMS = pltpu.CompilerParams(vmem_limit_bytes=24 << 20)


def on_core(kernel, out_shape, *operands):
    return pl.pallas_call(
        kernel,
        out_shape=out_shape,
        in_specs=[VMEM] * len(operands),
        out_specs=VMEM,
        compiler_params=PARAMS,
    )(*operands)


def in_order(kernel, out_shape, *operands):
    n = len(operands)
    later = operands[-1]
    return pl.pallas_call(
        kernel,
        out_shape=[out_shape, jax.ShapeDtypeStruct(later.shape, later.dtype)],
        in_specs=[VMEM] * (n - 1) + [ANY],
        out_specs=[VMEM, ANY],
        input_output_aliases={n - 1: 1},
        compiler_params=PARAMS,
    )(*operands)


SMEM = pl.BlockSpec(memory_space=pltpu.SMEM)


def with_scalars(kernel, out_shape, scalars, *operands):
    return pl.pallas_call(
        kernel,
        out_shape=out_shape,
        in_specs=[SMEM] + [VMEM] * len(operands),
        out_specs=[VMEM] * len(out_shape),
        compiler_params=PARAMS,
    )(scalars, *operands)


def partials_kernel(plane_ref, up_ref, down_ref, *refs):
    parts_ref, inputs_ref, upstream_ref = refs[-3:]
    for array, (weight_ref, rows_ref) in enumerate(
        ((up_ref, inputs_ref), (down_ref, upstream_ref))
    ):
        rows = plane_ref[:, array].reshape(256, -1)
        rows_ref[...] = rows
        both = lax.dot_general(
            weight_ref[...],
            rows,
            (((array,), (1,)), ((), ())),
            preferred_element_type=jnp.float32,
        ).astype(jnp.bfloat16)
        for block in range(2):
            parts_ref[block, array] = both[:, 128 * block : 128 * block + 128]


def partials(half, plane, up_weight, down_weight, *so_far):
    features, hidden = up_weight.shape
    return pl.pallas_call(
        partials_kernel,
        grid=(1,),
        out_shape=[
            jax.ShapeDtypeStruct((4, 2, hidden, 128), jnp.bfloat16),
            pltpu.HBM((512, features), jnp.bfloat16),
            pltpu.HBM((512, features), jnp.bfloat16),
        ],
        in_specs=[VMEM] * 3 + [ANY] * len(so_far),
        out_specs=[
            pl.BlockSpec((2, 2, hidden, 128), lambda i: (half, 0, 0, 0)),
            pl.BlockSpec((256, features), lambda i: (half, 0)),
            pl.BlockSpec((256, features), lambda i: (half, 0)),
        ],
        input_output_aliases={3 + i: i for i in range(len(so_far))},
        compiler_params=PARAMS,
        cost_estimate=pl.CostEstimate(
            flops=2 * 512 * features * hidden, bytes_accessed=4 << 20, transcendentals=0
        ),
    )(plane, up_weight, down_weight, *so_far)


def halve_kernel(bits_ref, staying_ref, arrived_ref, leaving_out, staying_out):
    near = bits_ref[0]
    for side, out_ref in ((1 - near, leaving_out), (near, staying_out)):
        both = staying_ref[side].astype(jnp.float32) + arrived_ref[side].astype(jnp.float32)
        out_ref[...] = both.astype(out_ref.dtype)


def token_grad_kernel(first, hidden_grad_ref, up_ref, *refs):
    out_ref = refs[-2] if len(refs) == 3 else refs[0]
    for piece in range(2):
        out_ref[pl.ds(128 * piece, 128)] = lax.dot_general(
            hidden_grad_ref[first + piece],
            up_ref[...],
            (((0,), (1,)), ((), ())),
            preferred_element_type=jnp.float32,
        ).astype(jnp.bfloat16)


def total_kernel(blocks_ref, out_ref):
    acc = blocks_ref[0].astype(jnp.float32)
    for i in range(1, blocks_ref.shape[0]):
        acc = acc + blocks_ref[i].astype(jnp.float32)
    out_ref[...] = acc.astype(jnp.bfloat16)


def add_kernel(*refs):
    acc = refs[0][...].astype(jnp.float32)
    for ref in refs[1:-1]:
        acc = acc + ref[...].astype(jnp.float32)
    refs[-1][...] = acc.astype(jnp.bfloat16)


def weight_grads_kernel(
    place_ref,
    inputs_ref,
    upstream_ref,
    hidden_grad_ref,
    *refs,
):
    parts, (up_out, down_out, active_ref, up_ref, down_ref, sems) = refs[:4], refs[4:]

    def whole(ref):
        return jnp.concatenate([ref[i] for i in range(4)], axis=1)

    copies = [
        pltpu.make_async_copy(up_ref, up_out, sems.at[0]),
        pltpu.make_async_copy(down_ref, down_out, sems.at[1]),
    ]
    up_ref[...] = lax.dot_general(
        inputs_ref[...],
        whole(hidden_grad_ref),
        (((0,), (1,)), ((), ())),
        preferred_element_type=jnp.float32,
    )
    copies[0].start()
    for k in range(4):
        active_ref[place_ref[0] ^ k] = parts[k][...]
    down_ref[...] = jnp.dot(
        whole(active_ref), upstream_ref[...], preferred_element_type=jnp.float32
    )
    copies[1].start()
    for copy in copies:
        copy.wait()


def weight_grads(place, inputs, upstream, hidden_grad, active_parts):
    tokens, features = inputs.shape
    hidden = hidden_grad.shape[1]
    up = (features, hidden)
    down = (hidden, features)
    return pl.pallas_call(
        weight_grads_kernel,
        out_shape=[pltpu.HBM(up, jnp.float32), pltpu.HBM(down, jnp.float32)],
        in_specs=[SMEM] + [VMEM] * 7,
        out_specs=[ANY, ANY],
        scratch_shapes=[
            pltpu.VMEM(hidden_grad.shape, jnp.bfloat16),
            pltpu.VMEM(up, jnp.float32),
            pltpu.VMEM(down, jnp.float32),
            pltpu.SemaphoreType.DMA((2,)),
        ],
        compiler_params=PARAMS,
        cost_estimate=pl.CostEstimate(
            flops=4 * tokens * features * hidden, bytes_accessed=8 << 20, transcendentals=0
        ),
    )(place.reshape(1), inputs, upstream, hidden_grad, *active_parts)


def on_device(tokens, out_grad, up_weight, down_weight):
    rows, features = tokens.shape
    hidden = up_weight.shape[1]

    def exchange(blocks, axis):
        return lax.all_to_all(blocks, axis, split_axis=0, concat_axis=0, tiled=True)

    def row_gather(part):
        return lax.all_gather(part[None], ("zb", "zc"), axis=0, tiled=True)

    with jax.named_scope("gather_tokens"):
        pair = lax.all_gather(jnp.stack([tokens, out_grad]), "far", axis=1, tiled=True)
        copies = jnp.broadcast_to(pair[None], (16,) + pair.shape)
        own = exchange(copies, ("x", "y"))
        other = lax.ppermute(own, "core", SWAP)
    with jax.named_scope("row_sums"):
        first = partials(0, own, up_weight, down_weight)
        parts, inputs, upstream = partials(1, other, up_weight, down_weight, *first)
        near, next_to = lax.axis_index("zb"), lax.axis_index("zc")
        bits = jnp.stack([near, next_to])
        pair = parts.reshape(2, 2, 2, hidden, 128)
        sums = []
        for array in range(2):
            leaving, staying = (
                lax.dynamic_index_in_dim(pair[:, :, array], side, 1, keepdims=False)
                for side in (1 - next_to, next_to)
            )
            leaving, staying = with_scalars(
                halve_kernel,
                [
                    jax.ShapeDtypeStruct((hidden, 128), jnp.bfloat16),
                    jax.ShapeDtypeStruct((hidden, 128), jnp.float32),
                ],
                bits,
                staying,
                lax.ppermute(leaving, "zc", SWAP),
            )
            mine = on_core(
                add_kernel,
                jax.ShapeDtypeStruct((hidden, 128), jnp.bfloat16),
                staying,
                lax.ppermute(leaving, "zb", SWAP),
            )
            theirs = lax.ppermute(mine, "za", SWAP)
            sums.append(mine.astype(jnp.float32) + theirs.astype(jnp.float32))
        preact, grad_active = sums
    with jax.named_scope("activate"):
        cdf = 0.5 * (1.0 + lax.erf(preact * 0.7071067811865476))
        slope = cdf + preact * jnp.exp(-0.5 * preact * preact) * 0.3989422804014327
        hidden_grad = row_gather((grad_active * slope).astype(jnp.bfloat16))
        active = (preact * cdf).astype(jnp.bfloat16)
    with jax.named_scope("token_grad"):
        half = jax.ShapeDtypeStruct((256, features), jnp.bfloat16)
        leaving, active = in_order(
            functools.partial(token_grad_kernel, 2), half, hidden_grad, up_weight, active
        )
        staying = on_core(functools.partial(token_grad_kernel, 0), half, hidden_grad, up_weight)
        arrived = lax.ppermute(leaving, "core", SWAP)
        chip_sum = on_core(add_kernel, half, staying, arrived)
        plane_sum = on_core(
            total_kernel,
            jax.ShapeDtypeStruct((2 * rows, features), jnp.bfloat16),
            exchange(chip_sum.reshape(16, -1, features), ("x", "y")),
        )
        far = lax.axis_index("far")
        mine, theirs = (
            lax.dynamic_slice_in_dim(plane_sum, rows * side, rows, axis=0)
            for side in (far, 1 - far)
        )
        token_grad = on_core(
            add_kernel,
            jax.ShapeDtypeStruct((rows, features), jnp.bfloat16),
            mine,
            lax.ppermute(theirs, "far", SWAP),
        )
    with jax.named_scope("weight_grads"):
        place = lax.axis_index(("zb", "zc"))
        active_parts = [active] + [
            lax.ppermute(active, ("zb", "zc"), [(i, i ^ k) for i in range(4)])
            for k in (1, 2, 3)
        ]
        up_grad, down_grad = weight_grads(place, inputs, upstream, hidden_grad, active_parts)
    return (token_grad, up_grad, down_grad)


def solution(mesh):
    fine = Mesh(mesh.devices.reshape(SIZES), AXES)
    return jax.shard_map(
        on_device,
        mesh=fine,
        in_specs=(P(TOKENS_OVER, ROW), P(TOKENS_OVER, ROW), P(ROW, TOKENS_OVER), P(TOKENS_OVER, ROW)),
        out_specs=(P(TOKENS_OVER, ROW), P(ROW, TOKENS_OVER), P(TOKENS_OVER, ROW)),
        check_vma=False,
    )
```

```python
import functools

import jax
import jax.numpy as jnp
from jax import lax
from jax.experimental import pallas as pl
from jax.experimental.pallas import tpu as pltpu
from jax.sharding import Mesh, PartitionSpec as P

AXES = ("za", "zb", "zc", "x", "core", "y", "far")
SIZES = (2, 2, 2, 4, 2, 4, 2)
ROW = ("za", "zb", "zc")
TOKENS_OVER = ("x", "core", "y", "far")
SWAP = [(0, 1), (1, 0)]


def gelu_cdf(preact):
    return 0.5 * (1.0 + lax.erf(preact * 0.7071067811865476))


VMEM = pl.BlockSpec(memory_space=pltpu.VMEM)
ANY = pl.BlockSpec(memory_space=pl.ANY)
PARAMS = pltpu.CompilerParams(vmem_limit_bytes=24 << 20)


def on_core(kernel, out_shape, *operands):
    return pl.pallas_call(
        kernel,
        out_shape=out_shape,
        in_specs=[VMEM] * len(operands),
        out_specs=VMEM,
        compiler_params=PARAMS,
    )(*operands)


def in_order(kernel, out_shape, *operands):
    n = len(operands)
    later = operands[-1]
    return pl.pallas_call(
        kernel,
        out_shape=[out_shape, jax.ShapeDtypeStruct(later.shape, later.dtype)],
        in_specs=[VMEM] * (n - 1) + [ANY],
        out_specs=[VMEM, ANY],
        input_output_aliases={n - 1: 1},
        compiler_params=PARAMS,
    )(*operands)


SMEM = pl.BlockSpec(memory_space=pltpu.SMEM)


def with_scalars(kernel, out_shape, scalars, *operands):
    return pl.pallas_call(
        kernel,
        out_shape=out_shape,
        in_specs=[SMEM] + [VMEM] * len(operands),
        out_specs=[VMEM] * len(out_shape),
        compiler_params=PARAMS,
    )(scalars, *operands)


def partials_kernel(arrays, plane_ref, *refs):
    weights, outs = refs[: len(arrays)], refs[-2 * len(arrays) :]
    for i, array in enumerate(arrays):
        rows = plane_ref[:, array].reshape(256, -1)
        outs[2 * i + 1][...] = rows
        both = lax.dot_general(
            weights[i][...],
            rows,
            (((array,), (1,)), ((), ())),
            preferred_element_type=jnp.float32,
        ).astype(jnp.bfloat16)
        for block in range(2):
            outs[2 * i][block] = both[:, 128 * block : 128 * block + 128]


def partials(half, arrays, plane, weights, so_far=()):
    features = plane.shape[3]
    hidden = weights[0].size // features
    first = 1 + len(weights)
    return pl.pallas_call(
        functools.partial(partials_kernel, arrays),
        grid=(1,),
        out_shape=[
            jax.ShapeDtypeStruct((4, hidden, 128), jnp.bfloat16),
            pltpu.HBM((512, features), jnp.bfloat16),
        ]
        * len(arrays),
        in_specs=[VMEM] * first + [ANY] * len(so_far),
        out_specs=[
            pl.BlockSpec((2, hidden, 128), lambda i: (half, 0, 0)),
            pl.BlockSpec((256, features), lambda i: (half, 0)),
        ]
        * len(arrays),
        input_output_aliases={first + i: i for i in range(len(so_far))},
        compiler_params=PARAMS,
        cost_estimate=pl.CostEstimate(
            flops=len(arrays) * 512 * features * hidden,
            bytes_accessed=len(arrays) << 21,
            transcendentals=0,
        ),
    )(plane, *weights, *so_far)


def halve_kernel(bits_ref, staying_ref, arrived_ref, leaving_out, staying_out):
    near = bits_ref[0]
    for side, out_ref in ((1 - near, leaving_out), (near, staying_out)):
        both = staying_ref[side].astype(jnp.float32) + arrived_ref[side].astype(jnp.float32)
        out_ref[...] = both.astype(out_ref.dtype)


def token_grad_kernel(first, hidden_grad_ref, up_ref, *refs):
    out_ref = refs[-2] if len(refs) == 3 else refs[0]
    for piece in range(2):
        out_ref[pl.ds(128 * piece, 128)] = lax.dot_general(
            hidden_grad_ref[first + piece],
            up_ref[...],
            (((0,), (1,)), ((), ())),
            preferred_element_type=jnp.float32,
        ).astype(jnp.bfloat16)


def total_kernel(blocks_ref, out_ref):
    acc = blocks_ref[0].astype(jnp.float32)
    for i in range(1, blocks_ref.shape[0]):
        acc = acc + blocks_ref[i].astype(jnp.float32)
    out_ref[...] = acc.astype(jnp.bfloat16)


def add_kernel(*refs):
    acc = refs[0][...].astype(jnp.float32)
    for ref in refs[1:-1]:
        acc = acc + ref[...].astype(jnp.float32)
    refs[-1][...] = acc.astype(jnp.bfloat16)


def weight_grads_kernel(
    place_ref,
    inputs_ref,
    upstream_ref,
    hidden_grad_ref,
    *refs,
):
    parts, (up_out, down_out, active_ref, up_ref, down_ref, sems) = refs[:4], refs[4:]

    def whole(ref):
        return jnp.concatenate([ref[i] for i in range(4)], axis=1)

    copies = [
        pltpu.make_async_copy(up_ref, up_out, sems.at[0]),
        pltpu.make_async_copy(down_ref, down_out, sems.at[1]),
    ]
    up_ref[...] = lax.dot_general(
        inputs_ref[...],
        whole(hidden_grad_ref),
        (((0,), (1,)), ((), ())),
        preferred_element_type=jnp.float32,
    )
    copies[0].start()
    for k in range(4):
        active_ref[place_ref[0] ^ k] = parts[k][...]
    down_ref[...] = jnp.dot(
        whole(active_ref), upstream_ref[...], preferred_element_type=jnp.float32
    )
    copies[1].start()
    for copy in copies:
        copy.wait()


def weight_grads(place, inputs, upstream, hidden_grad, active_parts):
    tokens, features = inputs.shape
    hidden = hidden_grad.shape[1]
    up = (features, hidden)
    down = (hidden, features)
    return pl.pallas_call(
        weight_grads_kernel,
        out_shape=[pltpu.HBM(up, jnp.float32), pltpu.HBM(down, jnp.float32)],
        in_specs=[SMEM] + [VMEM] * 7,
        out_specs=[ANY, ANY],
        scratch_shapes=[
            pltpu.VMEM(hidden_grad.shape, jnp.bfloat16),
            pltpu.VMEM(up, jnp.float32),
            pltpu.VMEM(down, jnp.float32),
            pltpu.SemaphoreType.DMA((2,)),
        ],
        compiler_params=PARAMS,
        cost_estimate=pl.CostEstimate(
            flops=4 * tokens * features * hidden, bytes_accessed=8 << 20, transcendentals=0
        ),
    )(place.reshape(1), inputs, upstream, hidden_grad, *active_parts)


def on_device(tokens, out_grad, up_weight, down_weight):
    rows, features = tokens.shape
    hidden = up_weight.shape[1]

    def exchange(blocks, axis):
        return lax.all_to_all(blocks, axis, split_axis=0, concat_axis=0, tiled=True)

    def row_gather(part):
        return lax.all_gather(part[None], ("zb", "zc"), axis=0, tiled=True)

    with jax.named_scope("gather_tokens"):
        pair = lax.all_gather(jnp.stack([tokens, out_grad]), "far", axis=1, tiled=True)
        copies = jnp.broadcast_to(pair[None], (16,) + pair.shape)
        own = exchange(copies, ("x", "y"))
        other = lax.ppermute(own, "core", SWAP)
    with jax.named_scope("row_sums"):
        weights = (up_weight, down_weight)
        begun = partials(0, (0, 1), own, weights)
        pre_parts, inputs = partials(1, (0,), other, weights[:1], begun[:2])
        grad_parts, upstream = partials(1, (1,), other, weights[1:], begun[2:])
        near, next_to = lax.axis_index("zb"), lax.axis_index("zc")
        bits = jnp.stack([near, next_to])
        sums = []
        for parts in (pre_parts, grad_parts):
            pair = parts.reshape(2, 2, hidden, 128)
            leaving, staying = (
                lax.dynamic_index_in_dim(pair, side, 1, keepdims=False)
                for side in (1 - next_to, next_to)
            )
            leaving, staying = with_scalars(
                halve_kernel,
                [
                    jax.ShapeDtypeStruct((hidden, 128), jnp.bfloat16),
                    jax.ShapeDtypeStruct((hidden, 128), jnp.float32),
                ],
                bits,
                staying,
                lax.ppermute(leaving, "zc", SWAP),
            )
            mine = on_core(
                add_kernel,
                jax.ShapeDtypeStruct((hidden, 128), jnp.bfloat16),
                staying,
                lax.ppermute(leaving, "zb", SWAP),
            )
            theirs = lax.ppermute(mine, "za", SWAP)
            sums.append(mine.astype(jnp.float32) + theirs.astype(jnp.float32))
        preact, grad_active = sums
    with jax.named_scope("activate"):
        cdf = 0.5 * (1.0 + lax.erf(preact * 0.7071067811865476))
        slope = cdf + preact * jnp.exp(-0.5 * preact * preact) * 0.3989422804014327
        hidden_grad = row_gather((grad_active * slope).astype(jnp.bfloat16))
        active = (preact * cdf).astype(jnp.bfloat16)
    with jax.named_scope("token_grad"):
        half = jax.ShapeDtypeStruct((256, features), jnp.bfloat16)
        leaving = on_core(
            functools.partial(token_grad_kernel, 2), half, hidden_grad, up_weight
        )
        staying, active = in_order(
            functools.partial(token_grad_kernel, 0), half, hidden_grad, up_weight, active
        )
        arrived = lax.ppermute(leaving, "core", SWAP)
        chip_sum = on_core(add_kernel, half, staying, arrived)
        plane_sum = on_core(
            total_kernel,
            jax.ShapeDtypeStruct((2 * rows, features), jnp.bfloat16),
            exchange(chip_sum.reshape(16, -1, features), ("x", "y")),
        )
        far = lax.axis_index("far")
        mine, theirs = (
            lax.dynamic_slice_in_dim(plane_sum, rows * side, rows, axis=0)
            for side in (far, 1 - far)
        )
        token_grad = on_core(
            add_kernel,
            jax.ShapeDtypeStruct((rows, features), jnp.bfloat16),
            mine,
            lax.ppermute(theirs, "far", SWAP),
        )
    with jax.named_scope("weight_grads"):
        place = lax.axis_index(("zb", "zc"))
        active_parts = [active] + [
            lax.ppermute(active, ("zb", "zc"), [(i, i ^ k) for i in range(4)])
            for k in (1, 2, 3)
        ]
        up_grad, down_grad = weight_grads(place, inputs, upstream, hidden_grad, active_parts)
    return (token_grad, up_grad, down_grad)


def solution(mesh):
    fine = Mesh(mesh.devices.reshape(SIZES), AXES)
    return jax.shard_map(
        on_device,
        mesh=fine,
        in_specs=(P(TOKENS_OVER, ROW), P(TOKENS_OVER, ROW), P(ROW, TOKENS_OVER), P(TOKENS_OVER, ROW)),
        out_specs=(P(TOKENS_OVER, ROW), P(ROW, TOKENS_OVER), P(TOKENS_OVER, ROW)),
        check_vma=False,
    )
```

```python
import functools

import jax
import jax.numpy as jnp
from jax import lax
from jax.experimental import pallas as pl
from jax.experimental.pallas import tpu as pltpu
from jax.sharding import Mesh, PartitionSpec as P

AXES = ("za", "zb", "zc", "x", "core", "y", "far")
SIZES = (2, 2, 2, 4, 2, 4, 2)
ROW = ("za", "zb", "zc")
TOKENS_OVER = ("x", "core", "y", "far")
SWAP = [(0, 1), (1, 0)]


def gelu_cdf(preact):
    return 0.5 * (1.0 + lax.erf(preact * 0.7071067811865476))


VMEM = pl.BlockSpec(memory_space=pltpu.VMEM)
ANY = pl.BlockSpec(memory_space=pl.ANY)
PARAMS = pltpu.CompilerParams(vmem_limit_bytes=24 << 20)


def on_core(kernel, out_shape, *operands):
    return pl.pallas_call(
        kernel,
        out_shape=out_shape,
        in_specs=[VMEM] * len(operands),
        out_specs=VMEM,
        compiler_params=PARAMS,
    )(*operands)


def in_order(kernel, out_shape, *operands):
    n = len(operands)
    later = operands[-1]
    return pl.pallas_call(
        kernel,
        out_shape=[out_shape, jax.ShapeDtypeStruct(later.shape, later.dtype)],
        in_specs=[VMEM] * (n - 1) + [ANY],
        out_specs=[VMEM, ANY],
        input_output_aliases={n - 1: 1},
        compiler_params=PARAMS,
    )(*operands)


SMEM = pl.BlockSpec(memory_space=pltpu.SMEM)


def with_scalars(kernel, out_shape, scalars, *operands):
    return pl.pallas_call(
        kernel,
        out_shape=out_shape,
        in_specs=[SMEM] + [VMEM] * len(operands),
        out_specs=[VMEM] * len(out_shape),
        compiler_params=PARAMS,
    )(scalars, *operands)


def partials_kernel(arrays, plane_ref, *refs):
    weights, outs = refs[: len(arrays)], refs[-2 * len(arrays) :]
    for i, array in enumerate(arrays):
        rows = plane_ref[:, array].reshape(256, -1)
        outs[2 * i + 1][...] = rows
        both = lax.dot_general(
            weights[i][...],
            rows,
            (((array,), (1,)), ((), ())),
            preferred_element_type=jnp.float32,
        ).astype(jnp.bfloat16)
        for block in range(2):
            outs[2 * i][block] = both[:, 128 * block : 128 * block + 128]


def partials(half, arrays, plane, weights, so_far=()):
    features = plane.shape[3]
    hidden = weights[0].size // features
    first = 1 + len(weights)
    return pl.pallas_call(
        functools.partial(partials_kernel, arrays),
        grid=(1,),
        out_shape=[
            jax.ShapeDtypeStruct((4, hidden, 128), jnp.bfloat16),
            pltpu.HBM((512, features), jnp.bfloat16),
        ]
        * len(arrays),
        in_specs=[VMEM] * first + [ANY] * len(so_far),
        out_specs=[
            pl.BlockSpec((2, hidden, 128), lambda i: (half, 0, 0)),
            pl.BlockSpec((256, features), lambda i: (half, 0)),
        ]
        * len(arrays),
        input_output_aliases={first + i: i for i in range(len(so_far))},
        compiler_params=PARAMS,
        cost_estimate=pl.CostEstimate(
            flops=len(arrays) * 512 * features * hidden,
            bytes_accessed=len(arrays) << 21,
            transcendentals=0,
        ),
    )(plane, *weights, *so_far)


def halve_kernel(bits_ref, staying_ref, arrived_ref, leaving_out, staying_out):
    near = bits_ref[0]
    for side, out_ref in ((1 - near, leaving_out), (near, staying_out)):
        both = staying_ref[side].astype(jnp.float32) + arrived_ref[side].astype(jnp.float32)
        out_ref[...] = both.astype(out_ref.dtype)


def token_grad_kernel(first, hidden_grad_ref, up_ref, *refs):
    out_ref = refs[-2] if len(refs) == 3 else refs[0]
    for piece in range(2):
        out_ref[pl.ds(128 * piece, 128)] = lax.dot_general(
            hidden_grad_ref[first + piece],
            up_ref[...],
            (((0,), (1,)), ((), ())),
            preferred_element_type=jnp.float32,
        ).astype(jnp.bfloat16)


def split_total_kernel(far_ref, blocks_ref, mine_ref, theirs_ref):
    acc = blocks_ref[0].astype(jnp.float32)
    for i in range(1, blocks_ref.shape[0]):
        acc = acc + blocks_ref[i].astype(jnp.float32)
    rows = mine_ref.shape[0]
    low, high, near = acc[:rows], acc[rows:], far_ref[0] == 0
    mine_ref[...] = jnp.where(near, low, high)
    theirs_ref[...] = jnp.where(near, high, low).astype(jnp.bfloat16)


def add_kernel(*refs):
    acc = refs[0][...].astype(jnp.float32)
    for ref in refs[1:-1]:
        acc = acc + ref[...].astype(jnp.float32)
    refs[-1][...] = acc.astype(jnp.bfloat16)


def weight_grads_kernel(
    place_ref,
    inputs_ref,
    upstream_ref,
    hidden_grad_ref,
    *refs,
):
    parts, (up_out, down_out, active_ref, up_ref, down_ref, sems) = refs[:4], refs[4:]

    def whole(ref):
        return jnp.concatenate([ref[i] for i in range(4)], axis=1)

    copies = [
        pltpu.make_async_copy(up_ref, up_out, sems.at[0]),
        pltpu.make_async_copy(down_ref, down_out, sems.at[1]),
    ]
    up_ref[...] = lax.dot_general(
        inputs_ref[...],
        whole(hidden_grad_ref),
        (((0,), (1,)), ((), ())),
        preferred_element_type=jnp.float32,
    )
    copies[0].start()
    for k in range(4):
        active_ref[place_ref[0] ^ k] = parts[k][...]
    down_ref[...] = jnp.dot(
        whole(active_ref), upstream_ref[...], preferred_element_type=jnp.float32
    )
    copies[1].start()
    for copy in copies:
        copy.wait()


def weight_grads(place, inputs, upstream, hidden_grad, active_parts):
    tokens, features = inputs.shape
    hidden = hidden_grad.shape[1]
    up = (features, hidden)
    down = (hidden, features)
    return pl.pallas_call(
        weight_grads_kernel,
        out_shape=[pltpu.HBM(up, jnp.float32), pltpu.HBM(down, jnp.float32)],
        in_specs=[SMEM] + [VMEM] * 7,
        out_specs=[ANY, ANY],
        scratch_shapes=[
            pltpu.VMEM(hidden_grad.shape, jnp.bfloat16),
            pltpu.VMEM(up, jnp.float32),
            pltpu.VMEM(down, jnp.float32),
            pltpu.SemaphoreType.DMA((2,)),
        ],
        compiler_params=PARAMS,
        cost_estimate=pl.CostEstimate(
            flops=4 * tokens * features * hidden, bytes_accessed=8 << 20, transcendentals=0
        ),
    )(place.reshape(1), inputs, upstream, hidden_grad, *active_parts)


def on_device(tokens, out_grad, up_weight, down_weight):
    rows, features = tokens.shape
    hidden = up_weight.shape[1]

    def exchange(blocks, axis):
        return lax.all_to_all(blocks, axis, split_axis=0, concat_axis=0, tiled=True)

    def row_gather(part):
        return lax.all_gather(part[None], ("zb", "zc"), axis=0, tiled=True)

    with jax.named_scope("gather_tokens"):
        pair = lax.all_gather(jnp.stack([tokens, out_grad]), "far", axis=1, tiled=True)
        copies = jnp.broadcast_to(pair[None], (16,) + pair.shape)
        own = exchange(copies, ("x", "y"))
        other = lax.ppermute(own, "core", SWAP)
    with jax.named_scope("row_sums"):
        weights = (up_weight, down_weight)
        begun = partials(0, (0, 1), own, weights)
        pre_parts, inputs = partials(1, (0,), other, weights[:1], begun[:2])
        grad_parts, upstream = partials(1, (1,), other, weights[1:], begun[2:])
        near, next_to = lax.axis_index("zb"), lax.axis_index("zc")
        bits = jnp.stack([near, next_to])
        sums = []
        for parts in (pre_parts, grad_parts):
            pair = parts.reshape(2, 2, hidden, 128)
            leaving, staying = (
                lax.dynamic_index_in_dim(pair, side, 1, keepdims=False)
                for side in (1 - next_to, next_to)
            )
            leaving, staying = with_scalars(
                halve_kernel,
                [
                    jax.ShapeDtypeStruct((hidden, 128), jnp.bfloat16),
                    jax.ShapeDtypeStruct((hidden, 128), jnp.float32),
                ],
                bits,
                staying,
                lax.ppermute(leaving, "zc", SWAP),
            )
            mine = on_core(
                add_kernel,
                jax.ShapeDtypeStruct((hidden, 128), jnp.bfloat16),
                staying,
                lax.ppermute(leaving, "zb", SWAP),
            )
            theirs = lax.ppermute(mine, "za", SWAP)
            sums.append(mine.astype(jnp.float32) + theirs.astype(jnp.float32))
        preact, grad_active = sums
    with jax.named_scope("activate"):
        cdf = 0.5 * (1.0 + lax.erf(preact * 0.7071067811865476))
        slope = cdf + preact * jnp.exp(-0.5 * preact * preact) * 0.3989422804014327
        hidden_grad = row_gather((grad_active * slope).astype(jnp.bfloat16))
        active = (preact * cdf).astype(jnp.bfloat16)
    with jax.named_scope("token_grad"):
        half = jax.ShapeDtypeStruct((256, features), jnp.bfloat16)
        leaving = on_core(
            functools.partial(token_grad_kernel, 2), half, hidden_grad, up_weight
        )
        staying, active = in_order(
            functools.partial(token_grad_kernel, 0), half, hidden_grad, up_weight, active
        )
        arrived = lax.ppermute(leaving, "core", SWAP)
        chip_sum = on_core(add_kernel, half, staying, arrived)
        mine, theirs = with_scalars(
            split_total_kernel,
            [
                jax.ShapeDtypeStruct((rows, features), jnp.float32),
                jax.ShapeDtypeStruct((rows, features), jnp.bfloat16),
            ],
            lax.axis_index("far").reshape(1),
            exchange(chip_sum.reshape(16, -1, features), ("x", "y")),
        )
        token_grad = on_core(
            add_kernel,
            jax.ShapeDtypeStruct((rows, features), jnp.bfloat16),
            mine,
            lax.ppermute(theirs, "far", SWAP),
        )
    with jax.named_scope("weight_grads"):
        place = lax.axis_index(("zb", "zc"))
        active_parts = [active] + [
            lax.ppermute(active, ("zb", "zc"), [(i, i ^ k) for i in range(4)])
            for k in (1, 2, 3)
        ]
        up_grad, down_grad = weight_grads(place, inputs, upstream, hidden_grad, active_parts)
    return (token_grad, up_grad, down_grad)


def solution(mesh):
    fine = Mesh(mesh.devices.reshape(SIZES), AXES)
    return jax.shard_map(
        on_device,
        mesh=fine,
        in_specs=(P(TOKENS_OVER, ROW), P(TOKENS_OVER, ROW), P(ROW, TOKENS_OVER), P(TOKENS_OVER, ROW)),
        out_specs=(P(TOKENS_OVER, ROW), P(ROW, TOKENS_OVER), P(TOKENS_OVER, ROW)),
        check_vma=False,
    )
```
